32 devices in a mesh: seq: 8 (over y, x, core), head: 4 (over z).
Axes of the slice: x: 2, y: 2, z: 4, core: 2. Of those that a mesh axis runs over, the one named last changes fastest.
Arguments:
- queries: bfloat16 [4096, 2048], P(('seq', 'head')), may hold values from -6 to 6
- keys: bfloat16 [4096, 2048], P(('seq', 'head')), may hold values from -6 to 6
- values: bfloat16 [4096, 2048], P(('seq', 'head')), may hold values from -6 to 6
- log_decay: bfloat16 [4096, 16], P(('seq', 'head')), may hold values from -0.6 to 0, as said below
- out_weight: bfloat16 [2048, 2048], P(('seq', 'head')), may hold values from -0.125 to 0.125
Outputs:
- mixed_out: bfloat16 [4096, 2048], P(('seq', 'head'))
The draws below stay inside these ranges and needn't reach their ends.
Inputs may be any that keep to these rules, and one draw needn't show every extreme that they name: `log_decay`: every entry is at most zero.
All inputs are finite; a program needn't handle non-finite values.
Results may differ from the reference program's by a relative error of at most 0.0054.
Values may be sent and summed in bfloat16 or wider, within the bound.
A program may use at most 64 MiB of HBM per device.

```python
import math
import jax
import jax.numpy as jnp
from jax import lax

H = 16
HD = 128
D = 2048
SPAN = 256
TOKENS = 4096


def draw_log_decay(key, part):
    key_heads, key_rates, key_noise, key_spots, key_depth = jax.random.split(jax.random.fold_in(key, 11), 5)
    order = jax.random.permutation(key_heads, H)
    fast_count = H // 2
    is_fast = order < fast_count
    spread = jax.random.uniform(key_rates, (H,), jnp.float32, 0.0, 1.0)
    fast_rate = jnp.exp(math.log(1.0 / 60.0) + spread * math.log(3.0))
    slow_rate = jnp.exp(math.log(0.2) + spread * math.log(3.0)) / TOKENS
    rate = jnp.where(is_fast, fast_rate, slow_rate)
    noise = jnp.exp(jax.random.uniform(key_noise, (TOKENS, H), jnp.float32, -math.log(2.0), math.log(2.0)))
    spots = jax.random.randint(key_spots, (3,), 0, TOKENS)
    positions = lax_iota(TOKENS)
    struck = jnp.any(positions[:, None] == spots[None, :], axis=1)
    depth = jax.random.uniform(key_depth, (TOKENS, 1), jnp.float32, 0.22, 0.5)
    result = -(rate[None, :] * noise) - jnp.where(struck[:, None], depth, 0.0)
    return result.astype(jnp.bfloat16)


def lax_iota(length):
    return jnp.arange(length, dtype=jnp.int32)


def shard_levels(key, shape, cuts, least, top_value):
    gain = 1.0
    for position, shards_of in cuts:
        heights = jax.random.uniform(jax.random.fold_in(jax.random.fold_in(key, 6), position), (shards_of,), jnp.float32, least / len(cuts), top_value / len(cuts))
        gain = gain * jnp.repeat(jnp.exp(heights), shape[position] // shards_of).reshape((-1,) + (1,) * (len(shape) - 1 - position))
    return gain


def bell_draw(stream_key, shape, width, bound, cuts=(), kind=jnp.bfloat16):
    entries = width * jax.random.normal(stream_key, shape, jnp.float32)
    if cuts:
        entries = entries * shard_levels(stream_key, shape, cuts, -0.22, 0.18)
    return jnp.clip(entries, -bound, bound).astype(kind)


def setup_inputs(seed: int = 0) -> dict:
    splits = jax.random.split(jax.random.key(seed), 6)
    queries = bell_draw(splits[0], (TOKENS, D), 1.0, 6.0, ((0, 32),))
    keys = bell_draw(splits[1], (TOKENS, D), 1.0, 6.0, ((0, 32),))
    values = bell_draw(splits[2], (TOKENS, D), 1.0, 6.0, ((0, 32),))
    log_decay = draw_log_decay(jax.random.fold_in(splits[5], 71), 0)
    out_weight = bell_draw(splits[4], (D, D), D ** -0.5, 0.125, ((0, 32),))
    return dict(queries=queries, keys=keys, values=values, log_decay=log_decay, out_weight=out_weight)


def reference(queries, keys, values, log_decay, out_weight):
    block_count = TOKENS // SPAN
    queries_blk = queries.reshape(block_count, SPAN, H, HD)
    keys_blk = keys.reshape(block_count, SPAN, H, HD)
    values_blk = values.reshape(block_count, SPAN, H, HD)
    decay_blk = log_decay.reshape(block_count, SPAN, H)
    causal = lax.broadcasted_iota(jnp.int32, (SPAN, SPAN), 0) >= lax.broadcasted_iota(jnp.int32, (SPAN, SPAN), 1)

    def advance(state_now, inputs):
        query_part, key_part, value_part, decay_part = inputs
        within = jnp.cumsum(decay_part.astype(jnp.float32), axis=0)
        block_decay = within[-1]
        within_t = within.T
        differences = within_t[:, :, None] - within_t[:, None, :]
        decay_mask = jnp.exp(jnp.where(causal[None], differences, -jnp.inf))
        query_f = query_part.astype(jnp.float32)
        key_f = key_part.astype(jnp.float32)
        value_f = value_part.astype(jnp.float32)
        scores = jnp.einsum('thd,shd->hts', query_f, key_f)
        weights = (scores * decay_mask).astype(jnp.bfloat16)
        local_part = jnp.einsum('hts,shd->thd', weights.astype(jnp.float32), value_f)
        scaled_keys = (jnp.exp(block_decay[None, :] - within)[:, :, None] * key_f).astype(jnp.bfloat16)
        block_state = jnp.einsum('shd,she->hde', scaled_keys.astype(jnp.float32), value_f)
        scaled_queries = query_f * jnp.exp(within)[:, :, None]
        carried_part = jnp.einsum('thd,hde->the', scaled_queries, state_now, precision=lax.Precision.HIGHEST)
        combined = local_part + carried_part
        normed = combined * lax.rsqrt(lax.optimization_barrier(jnp.mean(combined * combined, axis=-1, keepdims=True)) + 1e-05)
        state_next = jnp.exp(block_decay)[:, None, None] * state_now + block_state
        return (state_next, normed.astype(jnp.bfloat16))
    initial = jnp.zeros((H, HD, HD), jnp.float32)
    _, normed_all = lax.scan(advance, initial, (queries_blk, keys_blk, values_blk, decay_blk))
    normed_all = normed_all.reshape(TOKENS, D)
    return jnp.dot(normed_all, out_weight, preferred_element_type=jnp.float32).astype(jnp.bfloat16)
```

```python
import functools

import jax
import jax.numpy as jnp
from jax import lax
from jax.experimental import pallas as pl
from jax.experimental.pallas import tpu as pltpu
from jax.sharding import PartitionSpec as P

HD = 128
F32, BF16 = jnp.float32, jnp.bfloat16
MESH = pl.DeviceIdType.MESH


def contract(a, b, da, db):
    return lax.dot_general(a, b, (((da,), (db,)), ((), ())), preferred_element_type=F32)


def kernel(n_seq, n_head, heads, fused, *refs):
    if fused:
        q_ref, k_ref, v_ref, dec_ref, w_ref, o_ref = refs[:6]
        refs = refs[6:]
    else:
        q_ref, k_ref, v_ref, dec_ref, o_ref = refs[:5]
        refs = refs[5:]
    (st1, rc1, tb, rb, st3, rc3, pre, tot, inc, loc, s1s, s1r, s2s, s2r, s3s, s3r) = refs[:16]
    if fused:
        normed, wall, zup, zdn, zr, cxs, cxr, cys, cyr, ays, ayr, bxs, bxr, sbs, sbr = refs[16:]
    else:
        normed = o_ref
    rows = q_ref.shape[0]
    hg = heads // n_head
    span = hg * HD
    bits = n_seq.bit_length() - 1
    s, z = lax.axis_index("seq"), lax.axis_index("head")

    def flipped(k):
        bit = lax.rem(lax.div(s, 1 << k), 2)
        return s + (1 - 2 * bit) * (1 << k), bit

    def remote(src, dst, ssem, rsem, to):
        return pltpu.make_async_remote_copy(
            src_ref=src, dst_ref=dst, send_sem=ssem, recv_sem=rsem, device_id=to, device_id_type=MESH
        )

    barrier = pltpu.get_barrier_semaphore()
    for off in range(1, n_head):
        pl.semaphore_signal(barrier, inc=1, device_id=(s, lax.rem(z + off, n_head)), device_id_type=MESH)
    for k in range(bits):
        pl.semaphore_signal(barrier, inc=1, device_id=(flipped(k)[0], z), device_id_type=MESH)
    pl.semaphore_wait(barrier, n_head - 1 + bits)

    if fused:
        half = wall.shape[1]
        sib, sx, sy = (flipped(k)[0] for k in range(3))
        sxy = sx + sy - s

        def block(seq, zz):
            return wall.at[pl.ds(2 * (seq * n_head + zz), 2)]

        def part(seq, zz, which):
            return wall.at[2 * (seq * n_head + zz) + which]

        def up(zz):
            return remote(block(s, zz), block(s, zz), zup.at[zz], zr.at[zz], (s, z + 1))

        def down(zz):
            return remote(block(s, zz), block(s, zz), zdn.at[zz], zr.at[zz], (s, z - 1))

        def to_x(seq, zz):
            return remote(block(seq, zz), block(seq, zz), cxs.at[zz], cxr.at[zz], (sx, z))

        def to_y(seq, zz):
            return remote(block(seq, zz), block(seq, zz), cys.at[zz], cyr.at[zz], (sy, z))

        def a_to_y(seq, zz):
            return remote(part(seq, zz, 0), part(seq, zz, 0), ays.at[zz], ayr.at[zz], (sy, z))

        def b_to_x(seq, zz):
            return remote(part(seq, zz, 1), part(seq, zz, 1), bxs.at[zz], bxr.at[zz], (sx, z))

        def to_sib(kind, seq, zz):
            return remote(block(seq, zz), block(seq, zz), sbs.at[kind, zz], sbr.at[kind, zz], (sib, z))

        def near(j, body):
            if j == 0:
                body(z, 0)
                return
            pl.when(z - j >= 0)(lambda: body(z - j, 1))
            pl.when(z + j < n_head)(lambda: body(z + j, -1))

        def column(zz, way):
            if way:
                up(zz).wait_recv()
            if way >= 0:
                pl.when(z + 1 < n_head)(lambda: up(zz).start())
            if way <= 0:
                pl.when(z >= 1)(lambda: down(zz).start())
            to_x(s, zz).start()
            to_y(s, zz).start()
            to_sib(0, s, zz).start()

        def second(zz, way):
            to_x(sx, zz).wait_recv()
            a_to_y(sx, zz).start()
            to_sib(1, sx, zz).start()
            to_y(sy, zz).wait_recv()
            b_to_x(sy, zz).start()
            to_sib(2, sy, zz).start()

        def third(zz, way):
            a_to_y(sxy, zz).wait_recv()
            b_to_x(sxy, zz).wait_recv()
            to_sib(3, sxy, zz).start()

        mine = 2 * (s * n_head + z)
        wall[mine] = w_ref[:half]
        wall[mine + 1] = w_ref[half:]
        near(0, column)

    row_id = lax.broadcasted_iota(jnp.int32, (rows, rows), 0)
    col_id = lax.broadcasted_iota(jnp.int32, (rows, rows), 1)
    causal = row_id >= col_id
    dec = dec_ref[...]
    within = contract(causal.astype(F32).astype(BF16), dec, 1, 0)
    within_t = contract(dec, (row_id <= col_id).astype(F32).astype(BF16), 0, 0)
    key_scale = jnp.exp(within[rows - 1 : rows, :] - within)
    query_scale = jnp.exp(within)
    tile_row = lax.broadcasted_iota(jnp.int32, (16, HD), 0)

    def put_decays(ref, slot, decays):
        tile = jnp.zeros((16, HD), F32)
        for j, d in enumerate(decays):
            high = d.astype(BF16).astype(F32)
            tile = jnp.where(tile_row == 2 * j, high, tile)
            tile = jnp.where(tile_row == 2 * j + 1, d - high, tile)
        ref[slot, span : span + 16, :] = tile.astype(BF16)

    def get_decays(ref, slot):
        tile = ref[slot, span : span + 16, :].astype(F32)
        return [tile[2 * j : 2 * j + 1] + tile[2 * j + 1 : 2 * j + 2] for j in range(hg)]

    for g in range(n_head):
        decays = []
        for j in range(hg):
            h = g * hg + j
            at = slice(h * HD, (h + 1) * HD)
            scaled = (key_scale[:, h : h + 1] * k_ref[:, at].astype(F32)).astype(BF16)
            st1[g, j * HD : (j + 1) * HD, :] = contract(scaled, v_ref[:, at], 0, 0).astype(BF16)
            decays.append(jnp.broadcast_to(within_t[h : h + 1, rows - 1 : rows], (1, HD)))
        put_decays(st1, g, decays)

    def first(off):
        to = lax.rem(z + off, n_head)
        return remote(st1.at[to], rc1.at[z], s1s.at[off], s1r.at[z], (s, to))

    for off in range(1, n_head):
        first(off).start()
    rc1[z] = st1[z]

    def local(some):
        for h in some:
            at = slice(h * HD, (h + 1) * HD)
            gaps = within[:, h : h + 1] - within_t[h : h + 1, :]
            mask = jnp.exp(jnp.where(causal, gaps, -jnp.inf))
            weights = (contract(q_ref[:, at], k_ref[:, at], 1, 1) * mask).astype(BF16)
            loc[:, at] = contract(weights, v_ref[:, at], 1, 0)

    local(range(heads // 2))
    if fused:
        near(1, column)
    local(range(heads // 2, heads))
    if fused:
        near(2, column)
        near(0, second)

    for off in range(1, n_head):
        frm = lax.rem(z + off, n_head)
        remote(st1.at[frm], rc1.at[frm], s1s.at[off], s1r.at[frm], (s, frm)).wait_recv()
    arrived = [get_decays(rc1, zz) for zz in range(n_head)]
    before = [[jnp.zeros((1, HD), F32)] * hg]
    for zz in range(n_head):
        before.append([a + b for a, b in zip(before[-1], arrived[zz])])
    for j in range(hg):
        at = slice(j * HD, (j + 1) * HD)
        run = jnp.zeros((HD, HD), F32)
        for zz in range(n_head):
            pre[zz, at, :] = run
            run = jnp.exp(arrived[zz][j]) * run + rc1[zz, at, :].astype(F32)
        tot[at, :] = run
    inc[...] = jnp.zeros_like(inc)
    total = before[n_head]
    entering = [jnp.zeros((1, HD), F32)] * hg
    for k in range(bits):
        partner, bit = flipped(k)
        tb[k, :span, :] = tot[...].astype(BF16)
        put_decays(tb, k, total)
        swap = remote(tb.at[k], rb.at[k], s2s.at[k], s2r.at[k], (partner, z))
        swap.start()
        swap.wait_recv()
        theirs = get_decays(rb, k)
        later = jnp.broadcast_to(bit, (1, HD)) > 0
        for j in range(hg):
            at = slice(j * HD, (j + 1) * HD)
            other, own = rb[k, at, :].astype(F32), tot[at, :]
            take = jnp.where(later, jnp.exp(entering[j]), 0.0)
            inc[at, :] = inc[at, :] + take * other
            mine_scale = jnp.where(later, 1.0, jnp.exp(theirs[j]))
            other_scale = jnp.where(later, jnp.exp(total[j]), 1.0)
            tot[at, :] = mine_scale * own + other_scale * other
        entering = [jnp.where(later, a + b, a) for a, b in zip(entering, theirs)]
        total = [a + b for a, b in zip(total, theirs)]

    for zz in range(n_head):
        for j in range(hg):
            at = slice(j * HD, (j + 1) * HD)
            st3[zz, at, :] = (jnp.exp(before[zz][j]) * inc[at, :] + pre[zz, at, :]).astype(BF16)

    def last(off):
        to = lax.rem(z + off, n_head)
        return remote(st3.at[to], rc3.at[z], s3s.at[off], s3r.at[z], (s, to))

    for off in range(1, n_head):
        last(off).start()
    rc3[z] = st3[z]
    if fused:
        for j in range(3, n_head):
            near(j, column)
        for j in range(1, n_head):
            near(j, second)
        for j in range(n_head):
            near(j, third)

    for off in range(1, n_head):
        frm = lax.rem(z + off, n_head)
        remote(st3.at[frm], rc3.at[frm], s3s.at[off], s3r.at[frm], (s, frm)).wait_recv()
    for h in range(heads):
        at = slice(h * HD, (h + 1) * HD)
        j = h % hg
        scaled = (q_ref[:, at].astype(F32) * query_scale[:, h : h + 1]).astype(BF16)
        combined = loc[:, at] + contract(scaled, rc3[h // hg, j * HD : (j + 1) * HD, :], 1, 0)
        mean = jnp.mean(combined * combined, axis=-1, keepdims=True)
        normed[:, at] = (combined * lax.rsqrt(mean + 1e-05)).astype(BF16)

    if fused:
        for kind, flip in enumerate((sib, sib + sx - s, sib + sy - s, sib + sxy - s)):
            for zz in range(n_head):
                to_sib(kind, flip, zz).wait_recv()
        width = o_ref.shape[1]
        step = width // 4
        for c in range(0, width, step):
            w = wall[:, :, c : c + step].reshape(width, step)
            o_ref[:, c : c + step] = contract(normed[...], w, 1, 0).astype(BF16)
        for zz in range(n_head):
            pl.when((z >= zz) & (z + 1 < n_head))(lambda: up(zz).wait_send())
            pl.when((z <= zz) & (z >= 1))(lambda: down(zz).wait_send())
            to_x(s, zz).wait_send()
            to_y(s, zz).wait_send()
            a_to_y(sx, zz).wait_send()
            b_to_x(sy, zz).wait_send()
            for kind, seq in enumerate((s, sx, sy, sxy)):
                to_sib(kind, seq, zz).wait_send()
    for off in range(1, n_head):
        first(off).wait_send()
        last(off).wait_send()
    for k in range(bits):
        remote(tb.at[k], rb.at[k], s2s.at[k], s2r.at[k], (flipped(k)[0], z)).wait_send()


def local_part(queries, keys, values, log_decay, out_weight):
    n_seq, n_head = lax.axis_size("seq"), lax.axis_size("head")
    rows, width = queries.shape
    heads = log_decay.shape[1]
    bits = n_seq.bit_length() - 1
    span = heads // n_head * HD
    block = out_weight.shape[0]
    fused = n_seq == 8 and block % 32 == 0
    dma = pltpu.SemaphoreType.DMA
    scratch = [
        pltpu.VMEM((n_head, span + 16, HD), BF16),
        pltpu.VMEM((n_head, span + 16, HD), BF16),
        pltpu.VMEM((bits, span + 16, HD), BF16),
        pltpu.VMEM((bits, span + 16, HD), BF16),
        pltpu.VMEM((n_head, span, HD), BF16),
        pltpu.VMEM((n_head, span, HD), BF16),
        pltpu.VMEM((n_head, span, HD), F32),
        pltpu.VMEM((span, HD), F32),
        pltpu.VMEM((span, HD), F32),
        pltpu.VMEM((rows, width), F32),
        *(dma((n,)) for n in (n_head, n_head, bits, bits, n_head, n_head)),
    ]
    operands = [queries, keys, values, log_decay]
    if fused:
        operands.append(out_weight)
        scratch += [
            pltpu.VMEM((rows, width), BF16),
            pltpu.VMEM((2 * n_seq * n_head, block // 2, width), BF16),
            *(dma((n_head,)) for _ in range(11)),
            dma((4, n_head)),
            dma((4, n_head)),
        ]
    result = pl.pallas_call(
        functools.partial(kernel, n_seq, n_head, heads, fused),
        out_shape=jax.ShapeDtypeStruct((rows, width), BF16),
        in_specs=[pl.BlockSpec(memory_space=pltpu.VMEM)] * len(operands),
        out_specs=pl.BlockSpec(memory_space=pltpu.VMEM),
        scratch_shapes=scratch,
        compiler_params=pltpu.CompilerParams(
            collective_id=0, has_side_effects=True, vmem_limit_bytes=40 * 1024 * 1024
        ),
    )(*operands)
    if fused:
        return result
    weight = lax.all_gather(out_weight, ("seq", "head"), axis=0, tiled=True)
    return jnp.dot(result, weight, preferred_element_type=F32).astype(BF16)


def solution(mesh):
    placed = P(("seq", "head"), None)
    return jax.shard_map(
        local_part, mesh=mesh, in_specs=(placed,) * 5, out_specs=placed, check_vma=False
    )
```

```python
import functools

import jax
import jax.numpy as jnp
from jax import lax
from jax.experimental import pallas as pl
from jax.experimental.pallas import tpu as pltpu
from jax.sharding import PartitionSpec as P

HD = 128
F32, BF16 = jnp.float32, jnp.bfloat16
MESH = pl.DeviceIdType.MESH


def contract(a, b, da, db):
    return lax.dot_general(a, b, (((da,), (db,)), ((), ())), preferred_element_type=F32)


def kernel(n_seq, n_head, heads, fused, *refs):
    if fused:
        q_hbm, k_hbm, v_hbm, dec_hbm, w_hbm, o_ref = refs[:6]
        refs = refs[6:]
    else:
        q_hbm, k_hbm, v_hbm, dec_hbm, o_ref = refs[:5]
        refs = refs[5:]
    (q_ref, k_ref, v_ref, dec_ref, lds, st1, rc1, tb, rb, st3, rc3, pre, tot, inc, loc) = refs[:15]
    s1s, s1r, s2s, s2r, s3s, s3r = refs[15:21]
    if fused:
        normed, wall, zup, zdn, zr, cxs, cxr, cys, cyr, ays, ayr, bxs, bxr, sbs, sbr = refs[21:]
    else:
        normed = o_ref
    rows = q_ref.shape[0]
    batches = st1.shape[0]
    hg = heads // n_head // batches
    span = hg * HD
    bits = n_seq.bit_length() - 1
    s, z = lax.axis_index("seq"), lax.axis_index("head")

    def flipped(k):
        bit = lax.rem(lax.div(s, 1 << k), 2)
        return s + (1 - 2 * bit) * (1 << k), bit

    def remote(src, dst, ssem, rsem, to):
        return pltpu.make_async_remote_copy(
            src_ref=src, dst_ref=dst, send_sem=ssem, recv_sem=rsem, device_id=to, device_id_type=MESH
        )

    loads = [
        pltpu.make_async_copy(src, dst, lds.at[i])
        for i, (src, dst) in enumerate(((dec_hbm, dec_ref), (k_hbm, k_ref), (v_hbm, v_ref), (q_hbm, q_ref)))
    ]
    if fused:
        half = wall.shape[1]
        mine = 2 * (s * n_head + z)
        own = [
            pltpu.make_async_copy(w_hbm.at[pl.ds(i * half, half)], wall.at[mine + i], lds.at[4 + i])
            for i in range(2)
        ]
        for copy in own:
            copy.start()
    for copy in loads:
        copy.start()

    barrier = pltpu.get_barrier_semaphore()
    for off in range(1, n_head):
        pl.semaphore_signal(barrier, inc=1, device_id=(s, lax.rem(z + off, n_head)), device_id_type=MESH)
    for k in range(bits):
        pl.semaphore_signal(barrier, inc=1, device_id=(flipped(k)[0], z), device_id_type=MESH)
    pl.semaphore_wait(barrier, n_head - 1 + bits)

    if fused:
        sib, sx, sy = (flipped(k)[0] for k in range(3))
        sxy = sx + sy - s

        def block(seq, zz):
            return wall.at[pl.ds(2 * (seq * n_head + zz), 2)]

        def part(seq, zz, which):
            return wall.at[2 * (seq * n_head + zz) + which]

        def up(zz):
            return remote(block(s, zz), block(s, zz), zup.at[zz], zr.at[zz], (s, z + 1))

        def down(zz):
            return remote(block(s, zz), block(s, zz), zdn.at[zz], zr.at[zz], (s, z - 1))

        def to_x(seq, zz):
            return remote(block(seq, zz), block(seq, zz), cxs.at[zz], cxr.at[zz], (sx, z))

        def to_y(seq, zz):
            return remote(block(seq, zz), block(seq, zz), cys.at[zz], cyr.at[zz], (sy, z))

        def a_to_y(seq, zz):
            return remote(part(seq, zz, 0), part(seq, zz, 0), ays.at[zz], ayr.at[zz], (sy, z))

        def b_to_x(seq, zz):
            return remote(part(seq, zz, 1), part(seq, zz, 1), bxs.at[zz], bxr.at[zz], (sx, z))

        def to_sib(kind, seq, zz):
            return remote(block(seq, zz), block(seq, zz), sbs.at[kind, zz], sbr.at[kind, zz], (sib, z))

        def near(j, body):
            if j == 0:
                body(z, 0)
                return
            pl.when(z - j >= 0)(lambda: body(z - j, 1))
            pl.when(z + j < n_head)(lambda: body(z + j, -1))

        def column(zz, way):
            if way:
                up(zz).wait_recv()
            if way >= 0:
                pl.when(z + 1 < n_head)(lambda: up(zz).start())
            if way <= 0:
                pl.when(z >= 1)(lambda: down(zz).start())
            to_x(s, zz).start()
            to_y(s, zz).start()
            to_sib(0, s, zz).start()

        def second(zz, way):
            to_x(sx, zz).wait_recv()
            a_to_y(sx, zz).start()
            to_sib(1, sx, zz).start()
            to_y(sy, zz).wait_recv()
            b_to_x(sy, zz).start()
            to_sib(2, sy, zz).start()

        def third(zz, way):
            a_to_y(sxy, zz).wait_recv()
            b_to_x(sxy, zz).wait_recv()
            to_sib(3, sxy, zz).start()

        for copy in own:
            copy.wait()
        near(0, column)

    row_id = lax.broadcasted_iota(jnp.int32, (rows, rows), 0)
    col_id = lax.broadcasted_iota(jnp.int32, (rows, rows), 1)
    causal = row_id >= col_id
    loads[0].wait()
    dec = dec_ref[...]
    within = contract(causal.astype(F32).astype(BF16), dec, 1, 1)
    within_t = contract(dec, (row_id <= col_id).astype(F32).astype(BF16), 1, 0)
    key_scale = jnp.exp(within[rows - 1 : rows, :] - within)
    query_scale = jnp.exp(within)
    tile_row = lax.broadcasted_iota(jnp.int32, (16, HD), 0)

    def put_decays(ref, where, decays):
        tile = jnp.zeros((16, HD), F32)
        for j, d in enumerate(decays):
            high = d.astype(BF16).astype(F32)
            tile = jnp.where(tile_row == 2 * j, high, tile)
            tile = jnp.where(tile_row == 2 * j + 1, d - high, tile)
        ref[(*where, slice(span, span + 16), slice(None))] = tile.astype(BF16)

    def get_decays(ref, where):
        tile = ref[(*where, slice(span, span + 16), slice(None))].astype(F32)
        return [tile[2 * j : 2 * j + 1] + tile[2 * j + 1 : 2 * j + 2] for j in range(hg)]

    def head_of(b, g, j):
        return (g * batches + b) * hg + j

    def columns(h):
        return slice(h * HD, (h + 1) * HD)

    def state_rows(j):
        return slice(j * HD, (j + 1) * HD)

    def first(b, to, frm, off):
        return remote(st1.at[b, to], rc1.at[b, frm], s1s.at[b, off], s1r.at[b, frm], (s, to))

    def swap(b, k):
        return remote(tb.at[b, k], rb.at[b, k], s2s.at[b, k], s2r.at[b, k], (flipped(k)[0], z))

    def last(b, to, frm, off):
        return remote(st3.at[b, to], rc3.at[b, frm], s3s.at[b, off], s3r.at[b, frm], (s, to))

    def around(body):
        for off in range(1, n_head):
            body(lax.rem(z + off, n_head), off)

    def block_states(b):
        for g in range(n_head):
            decays = []
            for j in range(hg):
                h = head_of(b, g, j)
                scaled = (key_scale[:, h : h + 1] * k_ref[:, columns(h)].astype(F32)).astype(BF16)
                st1[b, g, state_rows(j), :] = contract(scaled, v_ref[:, columns(h)], 0, 0).astype(BF16)
                decays.append(jnp.broadcast_to(within_t[h : h + 1, rows - 1 : rows], (1, HD)))
            put_decays(st1, (b, g), decays)
        around(lambda to, off: first(b, to, z, off).start())
        rc1[b, z] = st1[b, z]

    def local(some):
        for h in some:
            at = columns(h)
            gaps = within[:, h : h + 1] - within_t[h : h + 1, :]
            mask = jnp.exp(jnp.where(causal, gaps, -jnp.inf))
            weights = (contract(q_ref[:, at], k_ref[:, at], 1, 1) * mask).astype(BF16)
            loc[:, at] = contract(weights, v_ref[:, at], 1, 0)

    before, total, entering = {}, {}, {}

    def send_total(b, k):
        tb[b, k, :span, :] = tot[b].astype(BF16)
        put_decays(tb, (b, k), total[b])
        swap(b, k).start()

    def over_head(b):
        around(lambda frm, off: first(b, frm, frm, off).wait_recv())
        arrived = [get_decays(rc1, (b, zz)) for zz in range(n_head)]
        sums = [[jnp.zeros((1, HD), F32)] * hg]
        for zz in range(n_head):
            sums.append([x + y for x, y in zip(sums[-1], arrived[zz])])
        for j in range(hg):
            at = state_rows(j)
            run = jnp.zeros((HD, HD), F32)
            for zz in range(n_head):
                pre[b, zz, at, :] = run
                run = jnp.exp(arrived[zz][j]) * run + rc1[b, zz, at, :].astype(F32)
            tot[b, at, :] = run
            inc[b, at, :] = jnp.zeros((HD, HD), F32)
        before[b], total[b], entering[b] = sums, sums[n_head], [jnp.zeros((1, HD), F32)] * hg
        send_total(b, 0)

    def over_seq(b, k):
        swap(b, k).wait_recv()
        later = jnp.broadcast_to(flipped(k)[1], (1, HD)) > 0
        theirs = get_decays(rb, (b, k))
        for j in range(hg):
            at = state_rows(j)
            other, ours = rb[b, k, at, :].astype(F32), tot[b, at, :]
            take = jnp.where(later, jnp.exp(entering[b][j]), 0.0)
            inc[b, at, :] = inc[b, at, :] + take * other
            ours_scale = jnp.where(later, 1.0, jnp.exp(theirs[j]))
            other_scale = jnp.where(later, jnp.exp(total[b][j]), 1.0)
            tot[b, at, :] = ours_scale * ours + other_scale * other
        entering[b] = [jnp.where(later, x + y, x) for x, y in zip(entering[b], theirs)]
        total[b] = [x + y for x, y in zip(total[b], theirs)]
        if k + 1 < bits:
            send_total(b, k + 1)
            return
        for zz in range(n_head):
            for j in range(hg):
                at = state_rows(j)
                st3[b, zz, at, :] = (jnp.exp(before[b][zz][j]) * inc[b, at, :] + pre[b, zz, at, :]).astype(BF16)
        around(lambda to, off: last(b, to, z, off).start())
        rc3[b, z] = st3[b, z]

    def finish(b):
        around(lambda frm, off: last(b, frm, frm, off).wait_recv())
        for g in range(n_head):
            for j in range(hg):
                h = head_of(b, g, j)
                at = columns(h)
                carried = contract(q_ref[:, at], rc3[b, g, state_rows(j), :], 1, 0)
                combined = loc[:, at] + query_scale[:, h : h + 1] * carried
                mean = jnp.mean(combined * combined, axis=-1, keepdims=True)
                normed[:, at] = (combined * lax.rsqrt(mean + 1e-05)).astype(BF16)

    relays = []
    if fused:
        relays = [(1, column), (0, second), (2, column), (1, second), (3, column), (2, second), (3, second)]
        relays += [(j, third) for j in range(n_head)]

    def relay(count=1):
        for _ in range(count):
            if relays:
                near(*relays.pop(0))

    loads[1].wait()
    loads[2].wait()
    for b in range(batches):
        block_states(b)
    loads[3].wait()
    local(range(heads // 2))
    relay()
    local(range(heads // 2, heads))
    for b in range(batches):
        over_head(b)
    for k in range(bits):
        for b in range(batches):
            relay()
            over_seq(b, k)
    relay(len(relays))
    for b in range(batches):
        finish(b)

    if fused:
        for kind, flip in enumerate((sib, sib + sx - s, sib + sy - s, sib + sxy - s)):
            for zz in range(n_head):
                to_sib(kind, flip, zz).wait_recv()
        width = o_ref.shape[1]
        step = width // 4
        for c in range(0, width, step):
            w = wall[:, :, c : c + step].reshape(width, step)
            o_ref[:, c : c + step] = contract(normed[...], w, 1, 0).astype(BF16)
        for zz in range(n_head):
            pl.when((z >= zz) & (z + 1 < n_head))(lambda: up(zz).wait_send())
            pl.when((z <= zz) & (z >= 1))(lambda: down(zz).wait_send())
            to_x(s, zz).wait_send()
            to_y(s, zz).wait_send()
            a_to_y(sx, zz).wait_send()
            b_to_x(sy, zz).wait_send()
            for kind, seq in enumerate((s, sx, sy, sxy)):
                to_sib(kind, seq, zz).wait_send()
    for b in range(batches):
        around(lambda to, off: first(b, to, z, off).wait_send())
        for k in range(bits):
            swap(b, k).wait_send()
        around(lambda to, off: last(b, to, z, off).wait_send())


def local_part(queries, keys, values, log_decay, out_weight):
    n_seq, n_head = lax.axis_size("seq"), lax.axis_size("head")
    rows, width = queries.shape
    heads = log_decay.shape[1]
    bits = n_seq.bit_length() - 1
    batches = 2 if heads // n_head % 2 == 0 else 1
    span = heads // n_head // batches * HD
    block = out_weight.shape[0]
    fused = n_seq == 8 and block % 32 == 0
    dma = pltpu.SemaphoreType.DMA
    scratch = [
        *(pltpu.VMEM((rows, width), BF16) for _ in range(3)),
        pltpu.VMEM((heads, rows), BF16),
        dma((6,)),
        pltpu.VMEM((batches, n_head, span + 16, HD), BF16),
        pltpu.VMEM((batches, n_head, span + 16, HD), BF16),
        pltpu.VMEM((batches, bits, span + 16, HD), BF16),
        pltpu.VMEM((batches, bits, span + 16, HD), BF16),
        pltpu.VMEM((batches, n_head, span, HD), BF16),
        pltpu.VMEM((batches, n_head, span, HD), BF16),
        pltpu.VMEM((batches, n_head, span, HD), F32),
        pltpu.VMEM((batches, span, HD), F32),
        pltpu.VMEM((batches, span, HD), F32),
        pltpu.VMEM((rows, width), F32),
        *(dma((batches, n)) for n in (n_head, n_head, bits, bits, n_head, n_head)),
    ]
    operands = [queries, keys, values, log_decay.T]
    if fused:
        operands.append(out_weight)
        scratch += [
            pltpu.VMEM((rows, width), BF16),
            pltpu.VMEM((2 * n_seq * n_head, block // 2, width), BF16),
            *(dma((n_head,)) for _ in range(11)),
            dma((4, n_head)),
            dma((4, n_head)),
        ]
    result = pl.pallas_call(
        functools.partial(kernel, n_seq, n_head, heads, fused),
        out_shape=jax.ShapeDtypeStruct((rows, width), BF16),
        in_specs=[pl.BlockSpec(memory_space=pltpu.HBM)] * len(operands),
        out_specs=pl.BlockSpec(memory_space=pltpu.VMEM),
        scratch_shapes=scratch,
        compiler_params=pltpu.CompilerParams(
            collective_id=0, has_side_effects=True, vmem_limit_bytes=40 * 1024 * 1024
        ),
    )(*operands)
    if fused:
        return result
    weight = lax.all_gather(out_weight, ("seq", "head"), axis=0, tiled=True)
    return jnp.dot(result, weight, preferred_element_type=F32).astype(BF16)


def solution(mesh):
    placed = P(("seq", "head"), None)
    return jax.shard_map(
        local_part, mesh=mesh, in_specs=(placed,) * 5, out_specs=placed, check_vma=False
    )
```

```python
import functools

import jax
import jax.numpy as jnp
from jax import lax
from jax.experimental import pallas as pl
from jax.experimental.pallas import tpu as pltpu
from jax.sharding import PartitionSpec as P

HD = 128
F32, BF16 = jnp.float32, jnp.bfloat16
MESH = pl.DeviceIdType.MESH
ORDER = (
    "L0", "L1", "X0", "H0", "C2", "H1", "S00", "S01", "X1", "S10",
    "S11", "C3", "S20", "S21", "X2", "X3", "T0", "T1", "T2", "F0",
    "F1", "P0", "P1", "T3", "P2", "P3", "P4", "P5", "P6", "P7",
)


def contract(a, b, da, db):
    return lax.dot_general(a, b, (((da,), (db,)), ((), ())), preferred_element_type=F32)


def kernel(n_seq, n_head, heads, fused, *refs):
    if fused:
        q_hbm, k_hbm, v_hbm, dec_hbm, w_hbm, o_ref = refs[:6]
        refs = refs[6:]
    else:
        q_hbm, k_hbm, v_hbm, dec_hbm, o_ref = refs[:5]
        refs = refs[5:]
    (q_ref, k_ref, v_ref, dec_ref, lds, st1, rc1, tb, rb, st3, rc3, pre, tot, inc, loc) = refs[:15]
    s1s, s1r, s2s, s2r, s3s, s3r = refs[15:21]
    if fused:
        normed, wall, zup, zdn, zr, cxs, cxr, cys, cyr, ays, ayr, bxs, bxr, sbs, sbr = refs[21:]
    else:
        normed = o_ref
    rows = q_ref.shape[0]
    batches = st1.shape[0]
    hg = heads // n_head // batches
    span = hg * HD
    bits = n_seq.bit_length() - 1
    s, z = lax.axis_index("seq"), lax.axis_index("head")

    def flipped(k):
        bit = lax.rem(lax.div(s, 1 << k), 2)
        return s + (1 - 2 * bit) * (1 << k), bit

    def remote(src, dst, ssem, rsem, to):
        return pltpu.make_async_remote_copy(
            src_ref=src, dst_ref=dst, send_sem=ssem, recv_sem=rsem, device_id=to, device_id_type=MESH
        )

    loads = [
        pltpu.make_async_copy(src, dst, lds.at[i])
        for i, (src, dst) in enumerate(((dec_hbm, dec_ref), (k_hbm, k_ref), (v_hbm, v_ref), (q_hbm, q_ref)))
    ]
    if fused:
        half = wall.shape[1]
        mine = 2 * (s * n_head + z)
        own = [
            pltpu.make_async_copy(w_hbm.at[pl.ds(i * half, half)], wall.at[mine + i], lds.at[4 + i])
            for i in range(2)
        ]
        for copy in own:
            copy.start()
    for copy in loads:
        copy.start()

    barrier = pltpu.get_barrier_semaphore()
    for off in range(1, n_head):
        pl.semaphore_signal(barrier, inc=1, device_id=(s, lax.rem(z + off, n_head)), device_id_type=MESH)
    for k in range(bits):
        pl.semaphore_signal(barrier, inc=1, device_id=(flipped(k)[0], z), device_id_type=MESH)
    pl.semaphore_wait(barrier, n_head - 1 + bits)

    if fused:
        sib, sx, sy = (flipped(k)[0] for k in range(3))
        sxy = sx + sy - s

        def block(seq, zz):
            return wall.at[pl.ds(2 * (seq * n_head + zz), 2)]

        def part(seq, zz, which):
            return wall.at[2 * (seq * n_head + zz) + which]

        def up(zz):
            return remote(block(s, zz), block(s, zz), zup.at[zz], zr.at[zz], (s, z + 1))

        def down(zz):
            return remote(block(s, zz), block(s, zz), zdn.at[zz], zr.at[zz], (s, z - 1))

        def to_x(seq, zz):
            return remote(block(seq, zz), block(seq, zz), cxs.at[zz], cxr.at[zz], (sx, z))

        def to_y(seq, zz):
            return remote(block(seq, zz), block(seq, zz), cys.at[zz], cyr.at[zz], (sy, z))

        def a_to_y(seq, zz):
            return remote(part(seq, zz, 0), part(seq, zz, 0), ays.at[zz], ayr.at[zz], (sy, z))

        def b_to_x(seq, zz):
            return remote(part(seq, zz, 1), part(seq, zz, 1), bxs.at[zz], bxr.at[zz], (sx, z))

        def to_sib(kind, seq, zz):
            return remote(block(seq, zz), block(seq, zz), sbs.at[kind, zz], sbr.at[kind, zz], (sib, z))

        def near(j, body):
            if j == 0:
                body(z, 0)
                return
            pl.when(z - j >= 0)(lambda: body(z - j, 1))
            pl.when(z + j < n_head)(lambda: body(z + j, -1))

        def column(zz, way):
            if way:
                up(zz).wait_recv()
            if way >= 0:
                pl.when(z + 1 < n_head)(lambda: up(zz).start())
            if way <= 0:
                pl.when(z >= 1)(lambda: down(zz).start())
            to_x(s, zz).start()
            to_y(s, zz).start()
            to_sib(0, s, zz).start()

        def second(zz, way):
            to_x(sx, zz).wait_recv()
            a_to_y(sx, zz).start()
            to_sib(1, sx, zz).start()
            to_y(sy, zz).wait_recv()
            b_to_x(sy, zz).start()
            to_sib(2, sy, zz).start()

        def third(zz, way):
            a_to_y(sxy, zz).wait_recv()
            b_to_x(sxy, zz).wait_recv()
            to_sib(3, sxy, zz).start()

        for copy in own:
            copy.wait()
        near(0, column)

    row_id = lax.broadcasted_iota(jnp.int32, (rows, rows), 0)
    col_id = lax.broadcasted_iota(jnp.int32, (rows, rows), 1)
    causal = row_id >= col_id
    loads[0].wait()
    dec = dec_ref[...]
    within = contract(causal.astype(F32).astype(BF16), dec, 1, 1)
    within_t = contract(dec, (row_id <= col_id).astype(F32).astype(BF16), 1, 0)
    key_scale = jnp.exp(within[rows - 1 : rows, :] - within)
    query_scale = jnp.exp(within)
    tile_row = lax.broadcasted_iota(jnp.int32, (16, HD), 0)

    def put_decays(ref, where, decays):
        tile = jnp.zeros((16, HD), F32)
        for j, d in enumerate(decays):
            high = d.astype(BF16).astype(F32)
            tile = jnp.where(tile_row == 2 * j, high, tile)
            tile = jnp.where(tile_row == 2 * j + 1, d - high, tile)
        ref[(*where, slice(span, span + 16), slice(None))] = tile.astype(BF16)

    def get_decays(ref, where):
        tile = ref[(*where, slice(span, span + 16), slice(None))].astype(F32)
        return [tile[2 * j : 2 * j + 1] + tile[2 * j + 1 : 2 * j + 2] for j in range(hg)]

    def head_of(b, g, j):
        return (g * batches + b) * hg + j

    def columns(h):
        return slice(h * HD, (h + 1) * HD)

    def state_rows(j):
        return slice(j * HD, (j + 1) * HD)

    def first(b, to, frm, off):
        return remote(st1.at[b, to], rc1.at[b, frm], s1s.at[b, off], s1r.at[b, frm], (s, to))

    def swap(b, k):
        return remote(tb.at[b, k], rb.at[b, k], s2s.at[b, k], s2r.at[b, k], (flipped(k)[0], z))

    def last(b, to, frm, off):
        return remote(st3.at[b, to], rc3.at[b, frm], s3s.at[b, off], s3r.at[b, frm], (s, to))

    def around(body):
        for off in range(1, n_head):
            body(lax.rem(z + off, n_head), off)

    def block_states(b):
        for g in range(n_head):
            decays = []
            for j in range(hg):
                h = head_of(b, g, j)
                scaled = (key_scale[:, h : h + 1] * k_ref[:, columns(h)].astype(F32)).astype(BF16)
                st1[b, g, state_rows(j), :] = contract(scaled, v_ref[:, columns(h)], 0, 0).astype(BF16)
                decays.append(jnp.broadcast_to(within_t[h : h + 1, rows - 1 : rows], (1, HD)))
            put_decays(st1, (b, g), decays)
        around(lambda to, off: first(b, to, z, off).start())
        rc1[b, z] = st1[b, z]

    def local(some):
        for h in some:
            at = columns(h)
            gaps = within[:, h : h + 1] - within_t[h : h + 1, :]
            mask = jnp.exp(jnp.where(causal, gaps, -jnp.inf))
            weights = (contract(q_ref[:, at], k_ref[:, at], 1, 1) * mask).astype(BF16)
            loc[:, at] = contract(weights, v_ref[:, at], 1, 0)

    before, total, entering = {}, {}, {}

    def send_total(b, k):
        tb[b, k, :span, :] = tot[b].astype(BF16)
        put_decays(tb, (b, k), total[b])
        swap(b, k).start()

    def over_head(b):
        around(lambda frm, off: first(b, frm, frm, off).wait_recv())
        arrived = [get_decays(rc1, (b, zz)) for zz in range(n_head)]
        sums = [[jnp.zeros((1, HD), F32)] * hg]
        for zz in range(n_head):
            sums.append([x + y for x, y in zip(sums[-1], arrived[zz])])
        for j in range(hg):
            at = state_rows(j)
            run = jnp.zeros((HD, HD), F32)
            for zz in range(n_head):
                pre[b, zz, at, :] = run
                run = jnp.exp(arrived[zz][j]) * run + rc1[b, zz, at, :].astype(F32)
            tot[b, at, :] = run
            inc[b, at, :] = jnp.zeros((HD, HD), F32)
        before[b], total[b], entering[b] = sums, sums[n_head], [jnp.zeros((1, HD), F32)] * hg
        send_total(b, 0)

    def over_seq(b, k):
        swap(b, k).wait_recv()
        later = jnp.broadcast_to(flipped(k)[1], (1, HD)) > 0
        theirs = get_decays(rb, (b, k))
        for j in range(hg):
            at = state_rows(j)
            other, ours = rb[b, k, at, :].astype(F32), tot[b, at, :]
            take = jnp.where(later, jnp.exp(entering[b][j]), 0.0)
            inc[b, at, :] = inc[b, at, :] + take * other
            ours_scale = jnp.where(later, 1.0, jnp.exp(theirs[j]))
            other_scale = jnp.where(later, jnp.exp(total[b][j]), 1.0)
            tot[b, at, :] = ours_scale * ours + other_scale * other
        entering[b] = [jnp.where(later, x + y, x) for x, y in zip(entering[b], theirs)]
        total[b] = [x + y for x, y in zip(total[b], theirs)]
        if k + 1 < bits:
            send_total(b, k + 1)
            return
        for zz in range(n_head):
            for j in range(hg):
                at = state_rows(j)
                st3[b, zz, at, :] = (jnp.exp(before[b][zz][j]) * inc[b, at, :] + pre[b, zz, at, :]).astype(BF16)
        around(lambda to, off: last(b, to, z, off).start())
        rc3[b, z] = st3[b, z]

    def finish(b):
        around(lambda frm, off: last(b, frm, frm, off).wait_recv())
        for g in range(n_head):
            for j in range(hg):
                h = head_of(b, g, j)
                at = columns(h)
                carried = contract(q_ref[:, at], rc3[b, g, state_rows(j), :], 1, 0)
                combined = loc[:, at] + query_scale[:, h : h + 1] * carried
                mean = jnp.mean(combined * combined, axis=-1, keepdims=True)
                normed[:, at] = (combined * lax.rsqrt(mean + 1e-05)).astype(BF16)

    def project(n):
        far, kind = n % 2, n // 2
        seq = (s, sx, sy, sxy)[kind]
        if far:
            seq = seq + sib - s
            for zz in range(n_head):
                to_sib(kind, seq, zz).wait_recv()
        width = o_ref.shape[1]
        deep = 2 * n_head * half
        left = normed[:, pl.ds(pl.multiple_of(seq * deep, deep), deep)]
        for c in range(0, width, width // 4):
            at = slice(c, c + width // 4)
            right = wall[pl.ds(seq * 2 * n_head, 2 * n_head), :, at].reshape(deep, width // 4)
            piece = contract(left, right, 1, 0)
            if n == 0:
                loc[:, at] = piece
            elif n < 7:
                loc[:, at] = loc[:, at] + piece
            else:
                o_ref[:, at] = (loc[:, at] + piece).astype(BF16)

    def run_step(step):
        kind, n = step[0], int(step[1:])
        if kind in "CXT":
            if fused:
                near(n, {"C": column, "X": second, "T": third}[kind]) if n < n_head else None
        elif kind == "P":
            project(n)
        elif kind == "L":
            local(range(n * heads // 2, (n + 1) * heads // 2))
        elif kind == "S":
            if n % 10 < batches:
                over_seq(n % 10, n // 10)
        elif n < batches:
            {"H": over_head, "F": finish}[kind](n)

    loads[1].wait()
    loads[2].wait()
    block_states(0)
    if fused:
        near(1, column)
    for b in range(1, batches):
        block_states(b)
    loads[3].wait()
    order = ORDER if fused else ["L0", "L1", "H0", "H1", *(f"S{k}{b}" for k in range(bits) for b in range(batches)), "F0", "F1"]
    for step in order:
        run_step(step)

    if fused:
        for zz in range(n_head):
            pl.when((z >= zz) & (z + 1 < n_head))(lambda: up(zz).wait_send())
            pl.when((z <= zz) & (z >= 1))(lambda: down(zz).wait_send())
            to_x(s, zz).wait_send()
            to_y(s, zz).wait_send()
            a_to_y(sx, zz).wait_send()
            b_to_x(sy, zz).wait_send()
            for kind, seq in enumerate((s, sx, sy, sxy)):
                to_sib(kind, seq, zz).wait_send()
    for b in range(batches):
        around(lambda to, off: first(b, to, z, off).wait_send())
        for k in range(bits):
            swap(b, k).wait_send()
        around(lambda to, off: last(b, to, z, off).wait_send())


def local_part(queries, keys, values, log_decay, out_weight):
    n_seq, n_head = lax.axis_size("seq"), lax.axis_size("head")
    rows, width = queries.shape
    heads = log_decay.shape[1]
    bits = n_seq.bit_length() - 1
    batches = 2 if heads // n_head % 2 == 0 else 1
    span = heads // n_head // batches * HD
    block = out_weight.shape[0]
    fused = n_seq == 8 and block % 32 == 0
    dma = pltpu.SemaphoreType.DMA
    scratch = [
        *(pltpu.VMEM((rows, width), BF16) for _ in range(3)),
        pltpu.VMEM((heads, rows), BF16),
        dma((6,)),
        pltpu.VMEM((batches, n_head, span + 16, HD), BF16),
        pltpu.VMEM((batches, n_head, span + 16, HD), BF16),
        pltpu.VMEM((batches, bits, span + 16, HD), BF16),
        pltpu.VMEM((batches, bits, span + 16, HD), BF16),
        pltpu.VMEM((batches, n_head, span, HD), BF16),
        pltpu.VMEM((batches, n_head, span, HD), BF16),
        pltpu.VMEM((batches, n_head, span, HD), F32),
        pltpu.VMEM((batches, span, HD), F32),
        pltpu.VMEM((batches, span, HD), F32),
        pltpu.VMEM((rows, width), F32),
        *(dma((batches, n)) for n in (n_head, n_head, bits, bits, n_head, n_head)),
    ]
    operands = [queries, keys, values, log_decay.T]
    if fused:
        operands.append(out_weight)
        scratch += [
            pltpu.VMEM((rows, width), BF16),
            pltpu.VMEM((2 * n_seq * n_head, block // 2, width), BF16),
            *(dma((n_head,)) for _ in range(11)),
            dma((4, n_head)),
            dma((4, n_head)),
        ]
    result = pl.pallas_call(
        functools.partial(kernel, n_seq, n_head, heads, fused),
        out_shape=jax.ShapeDtypeStruct((rows, width), BF16),
        in_specs=[pl.BlockSpec(memory_space=pltpu.HBM)] * len(operands),
        out_specs=pl.BlockSpec(memory_space=pltpu.VMEM),
        scratch_shapes=scratch,
        compiler_params=pltpu.CompilerParams(
            collective_id=0, has_side_effects=True, vmem_limit_bytes=40 * 1024 * 1024
        ),
    )(*operands)
    if fused:
        return result
    weight = lax.all_gather(out_weight, ("seq", "head"), axis=0, tiled=True)
    return jnp.dot(result, weight, preferred_element_type=F32).astype(BF16)


def solution(mesh):
    placed = P(("seq", "head"), None)
    return jax.shard_map(
        local_part, mesh=mesh, in_specs=(placed,) * 5, out_specs=placed, check_vma=False
    )
```
